128 devices in a mesh: boson: 16 (over x, y), row: 8 (over z, core).
Axes of the slice: x: 4, y: 4, z: 4, core: 2. Of those that a mesh axis runs over, the one named last changes fastest.
Arguments:
- vertex: bfloat16 [256, 1024, 1024], P('boson', 'row'), may hold values from -6 to 6
- bubble: float32 [256, 1024], P('boson'), may hold values from 0.004 to 0.04
- vertex_cross: bfloat16 [256, 1024, 1024], P('boson', 'row'), may hold values from -6 to 6
- crossing: int32 [256, 8], P('boson', 'row'), may hold values from 0 to 255, as said below
Outputs:
- ladder: bfloat16 [256, 1024, 1024], P('boson', 'row')
- crossed: bfloat16 [256, 1024, 1024], P('boson', 'row')
The draws below stay inside these ranges and needn't reach their ends.
Inputs may be any that keep to these rules, and one draw needn't show every extreme that they name: `crossing`: for each momentum block, the 16 bosonic indices of one aligned group send to the indices of any one aligned group of 16 either no block or exactly 2 blocks.
All inputs are finite; a program needn't handle non-finite values.
Results may differ from the reference program's by a relative error of at most 0.0075.
Values may be sent and summed in bfloat16 or wider, within the bound.
No kernel may reach another device: no remote copies, remote signals or barrier semaphores. Data moves between devices by JAX's collectives and lax.ppermute only.
A program may use at most 128 MiB of HBM per device.

```python
import math
import jax
import jax.numpy as jnp
from jax import lax

KB = 8
FREQ = 128
M = 1024
Q_DEV = 16
Q = 256
CAP = 2
ITERS = 6


def draw_crossing(key, part):
    key = jax.random.fold_in(key, 7)
    groups = Q // Q_DEV
    total = groups * KB

    def one_group(sub):
        first, second, third = jax.random.split(sub, 3)
        order = jax.random.permutation(first, Q_DEV)
        targets = jax.random.permutation(second, groups)
        device_of = targets[order // CAP]
        within = jax.random.randint(third, (Q_DEV,), 0, Q_DEV)
        return device_of * Q_DEV + within
    keys = jax.random.split(key, total)
    values = jax.vmap(one_group)(keys)
    values = values.reshape(groups, KB, Q_DEV)
    return jnp.transpose(values, (0, 2, 1)).reshape(Q, KB).astype(jnp.int32)


def level_of(own_key, extent, cuts, least, largest):
    def one(dim, shards_of):
        steps = jax.random.uniform(jax.random.fold_in(jax.random.fold_in(own_key, 6), dim), (shards_of,), jnp.float32, least / len(cuts), largest / len(cuts))
        return jnp.repeat(jnp.exp(steps), extent[dim] // shards_of).reshape((-1,) + (1,) * (len(extent) - dim - 1))

    factor_of = one(*cuts[0])
    for cut in cuts[1:]:
        factor_of = factor_of * one(*cut)
    return factor_of


def gaussian(key, dims, deviation, bound, cuts=(), dtype=jnp.bfloat16):
    level = level_of(key, dims, cuts, -0.22, 0.18) if cuts else 1.0
    drawn = jax.random.normal(key, dims, jnp.float32) * deviation * level
    return jnp.minimum(jnp.maximum(drawn, -bound), bound).astype(dtype)


def setup_inputs(seed: int = 0) -> dict:
    streams_of = jax.random.split(jax.random.key(seed), 5)
    vertex = gaussian(streams_of[0], (Q, M, M), 1.0, 6.0, ((0, 16), (1, 8)))
    bubble = jnp.clip(jnp.exp(math.log(0.04) - 2.30258502 * jax.random.uniform(streams_of[1], (Q, M), jnp.float32) ** level_of(streams_of[1], (Q, M), ((0, 16),), -0.2, 0.2)), 0.004, 0.04)
    vertex_cross = gaussian(streams_of[2], (Q, M, M), 1.0, 6.0, ((0, 16), (1, 8)))
    crossing = draw_crossing(jax.random.fold_in(streams_of[4], 71), 0)
    return dict(vertex=vertex, bubble=bubble, vertex_cross=vertex_cross, crossing=crossing)


def ladder_one(pair):
    matrix, scales = pair
    start = matrix.astype(jnp.float32)
    current = start
    for iteration in range(ITERS):
        scaled = (current * scales[None, :]).astype(jnp.bfloat16)
        current = start + jnp.dot(scaled, matrix, preferred_element_type=jnp.float32)
    return current.astype(jnp.bfloat16)


def reference(vertex, bubble, vertex_cross, crossing):
    ladder = lax.map(ladder_one, (vertex, bubble))
    pieces = []
    for block in range(KB):
        rows = ladder[:, block * FREQ:(block + 1) * FREQ, :].astype(jnp.float32)
        summed = jax.ops.segment_sum(rows, crossing[:, block], num_segments=Q)
        other = vertex_cross[:, block * FREQ:(block + 1) * FREQ, :].astype(jnp.float32)
        pieces.append((other + summed).astype(jnp.bfloat16))
    crossed = jnp.concatenate(pieces, axis=1)
    return ladder, crossed
```

```python
import functools

import jax
import jax.numpy as jnp
from jax import lax
from jax.experimental import pallas as pl
from jax.experimental.pallas import tpu as pltpu
from jax.sharding import PartitionSpec as P

CAP = 2
ITERS = 6
GROUP = 256


def sweep_kernel(vertex_ref, bubble_ref, ladder_ref):
    blocks, _, freq, width = vertex_ref.shape
    order = blocks * freq
    per_group = GROUP // freq
    scales = bubble_ref[0]

    @pl.loop(0, blocks // per_group)
    def _(group):
        rows = pl.ds(group * per_group, per_group)
        start = vertex_ref[rows, 0].reshape(GROUP, width).astype(jnp.float32)
        current = start
        for _ in range(ITERS):
            scaled = (current * scales).astype(jnp.bfloat16)
            matrix = vertex_ref[:, 0].reshape(order, width)
            current = start + jnp.dot(scaled, matrix, preferred_element_type=jnp.float32)
        ladder_ref[rows, 0] = current.astype(jnp.bfloat16).reshape(per_group, freq, width)


def sweeps(vertex, bubble):
    blocks, count, freq, width = vertex.shape
    block = pl.BlockSpec((blocks, 1, freq, width), lambda i: (0, i, 0, 0))
    return pl.pallas_call(
        sweep_kernel,
        grid=(count,),
        in_specs=[block, pl.BlockSpec((1, 1, width), lambda i: (i, 0, 0))],
        out_specs=block,
        out_shape=jax.ShapeDtypeStruct(vertex.shape, jnp.bfloat16),
        compiler_params=pltpu.CompilerParams(vmem_limit_bytes=48 << 20),
        cost_estimate=pl.CostEstimate(
            flops=2 * ITERS * count * width**3, bytes_accessed=8 * count * width**2, transcendentals=0
        ),
        name="sweeps",
    )(vertex, bubble.reshape(count, 1, width))


def pack_kernel(crossing_ref, ladder_ref, out_ref, used, sems):
    q_local = ladder_ref.shape[0]
    for slot in range(q_local):
        used[slot] = 0
    copies = []
    for index in range(q_local):
        target = crossing_ref[index] // q_local
        position = used[target]
        used[target] = position + 1
        copy = pltpu.make_async_copy(
            ladder_ref.at[index], out_ref.at[target * CAP + position], sems.at[index]
        )
        copy.start()
        copies.append(copy)
    for copy in copies:
        copy.wait()


def pack(crossing, ladder, slots):
    q_local, freq, width = ladder.shape
    return pl.pallas_call(
        pack_kernel,
        in_specs=[pl.BlockSpec(memory_space=pltpu.SMEM), pl.BlockSpec(memory_space=pl.ANY)],
        out_specs=pl.BlockSpec(memory_space=pl.ANY),
        out_shape=jax.ShapeDtypeStruct((slots, freq, width), jnp.bfloat16),
        scratch_shapes=[pltpu.SMEM((q_local,), jnp.int32), pltpu.SemaphoreType.DMA((q_local,))],
        name="pack",
    )(crossing, ladder)


def collect_kernel(ids_ref, incoming_ref, other_ref, out_ref, total):
    slots = incoming_ref.shape[0]
    total[...] = other_ref[...].astype(jnp.float32)

    @pl.loop(0, slots)
    def _(slot):
        target = ids_ref[slot]

        @pl.when(target >= 0)
        def _():
            total[target] += incoming_ref[slot].astype(jnp.float32)

    out_ref[...] = total[...].astype(jnp.bfloat16)


def collect(ids, incoming, other, step=16):
    slots, freq, width = incoming.shape
    q_local = other.shape[0]
    block = pl.BlockSpec((q_local, step, width), lambda i: (0, i, 0))
    return pl.pallas_call(
        collect_kernel,
        grid=(freq // step,),
        in_specs=[
            pl.BlockSpec(memory_space=pltpu.SMEM),
            pl.BlockSpec((slots, step, width), lambda i: (0, i, 0)),
            block,
        ],
        out_specs=block,
        out_shape=jax.ShapeDtypeStruct(other.shape, jnp.bfloat16),
        scratch_shapes=[pltpu.VMEM((q_local, step, width), jnp.float32)],
        compiler_params=pltpu.CompilerParams(vmem_limit_bytes=32 << 20),
        name="collect",
    )(ids, incoming, other)


def slot_targets(crossing, n_boson):
    q_local = crossing.shape[0]
    target_dev = crossing // q_local
    earlier = jnp.arange(q_local)[None, :] < jnp.arange(q_local)[:, None]
    position = jnp.sum((target_dev[:, None] == target_dev[None, :]) & earlier, axis=1, dtype=jnp.int32)
    slot_of = target_dev * CAP + position
    matches = slot_of[None, :] == jnp.arange(n_boson * CAP)[:, None]
    return jnp.max(jnp.where(matches, (crossing % q_local)[None, :], -1), axis=1)


def local(vertex, bubble, vertex_cross, crossing):
    n_boson, n_row = lax.axis_size("boson"), lax.axis_size("row")
    q_local, freq, width = vertex.shape
    mine = q_local // n_row
    slots = n_boson * CAP
    crossing = crossing.reshape(q_local)
    whole = lax.all_to_all(
        vertex.reshape(n_row, mine, freq, width), "row", split_axis=0, concat_axis=0, tiled=True
    )
    scales = lax.dynamic_slice_in_dim(bubble, lax.axis_index("row") * mine, mine, 0)
    solved = sweeps(whole, scales)
    ladder = lax.all_to_all(solved, "row", split_axis=0, concat_axis=0, tiled=True)
    ladder = ladder.reshape(q_local, freq, width)
    ids = slot_targets(crossing, n_boson)
    incoming_ids = lax.all_to_all(
        ids.reshape(n_boson, CAP), "boson", split_axis=0, concat_axis=0, tiled=True
    ).reshape(slots)
    outgoing = pack(crossing, ladder, slots)
    incoming = lax.all_to_all(
        outgoing.reshape(n_boson, CAP * freq, width), "boson", split_axis=0, concat_axis=0, tiled=True
    ).reshape(slots, freq, width)
    crossed = collect(incoming_ids, incoming, vertex_cross)
    return ladder, crossed


def solution(mesh):
    placed = (P("boson", "row", None), P("boson", None), P("boson", "row", None), P("boson", "row"))
    return jax.shard_map(
        local,
        mesh=mesh,
        in_specs=placed,
        out_specs=(P("boson", "row", None), P("boson", "row", None)),
        check_vma=False,
    )
```

```python
import functools

import jax
import jax.numpy as jnp
from jax import lax
from jax.experimental import pallas as pl
from jax.experimental.pallas import tpu as pltpu
from jax.sharding import PartitionSpec as P

CAP = 2
ITERS = 6
SIDE = 4
CHUNKS = (32, 48, 48)
AHEAD = 2
VMEM = pl.BlockSpec(memory_space=pltpu.VMEM)
SMEM = pl.BlockSpec(memory_space=pltpu.SMEM)
ANY = pl.BlockSpec(memory_space=pl.ANY)


def params(mib):
    return pltpu.CompilerParams(vmem_limit_bytes=mib << 20)


def cost(flops, nbytes):
    return pl.CostEstimate(flops=int(flops), bytes_accessed=int(nbytes), transcendentals=0)


def sweep_kernel(first, rows, vertex_ref, bubble_ref, ladder_ref):
    blocks, count, freq, width = vertex_ref.shape
    order = blocks * freq
    for index in range(count):
        scales = bubble_ref[index : index + 1, :]
        start = vertex_ref[:, index, first : first + rows].reshape(blocks * rows, width).astype(jnp.float32)
        current = start
        for _ in range(ITERS):
            scaled = (current * scales).astype(jnp.bfloat16)
            matrix = vertex_ref[:, index].reshape(order, width)
            current = start + jnp.dot(scaled, matrix, preferred_element_type=jnp.float32)
        ladder_ref[:, index] = current.astype(jnp.bfloat16).reshape(blocks, rows, width)


def sweeps(vertex, bubble, first, rows):
    blocks, count, freq, width = vertex.shape
    return pl.pallas_call(
        functools.partial(sweep_kernel, first, rows),
        in_specs=[VMEM, VMEM],
        out_specs=VMEM,
        out_shape=jax.ShapeDtypeStruct((blocks, count, rows, width), jnp.bfloat16),
        compiler_params=params(32),
        cost_estimate=cost(2 * ITERS * count * blocks * rows * width * width, 2 * vertex.size),
        name="sweeps",
    )(vertex, bubble)


def pack_kernel(first, rows, place_ref, crossing_ref, part_ref, *rest):
    ladder_ref, outs, used, sem = rest[-SIDE - 3], rest[-SIDE - 2 : -2], rest[-2], rest[-1]
    q_local = part_ref.shape[0]
    keep = pltpu.make_async_copy(part_ref, ladder_ref.at[:, first : first + rows], sem)
    keep.start()
    for slot in range(SIDE * SIDE * CAP):
        used[slot] = -1
    for index in range(q_local):
        target = crossing_ref[index] // q_local
        high, low = target // SIDE, target % SIDE
        swap = place_ref[2] == 1
        one = (jnp.where(swap, low, high) - place_ref[0] + SIDE) % SIDE
        two = (jnp.where(swap, high, low) - place_ref[1] + SIDE) % SIDE
        slot = (one * SIDE + two) * CAP
        slot = jnp.where(used[slot] < 0, slot, slot + 1)
        used[slot] = index
    for one in range(SIDE):
        for at in range(SIDE * CAP):
            index = used[one * SIDE * CAP + at]

            @pl.when(index >= 0)
            def _():
                outs[one][at] = part_ref[index]

    keep.wait()


def pack(place, crossing, part, ladder, first, freq):
    q_local, rows, width = part.shape
    slots = SIDE * SIDE * CAP
    whole = jax.ShapeDtypeStruct((q_local, freq, width), jnp.bfloat16)
    piece = jax.ShapeDtypeStruct((SIDE * CAP, rows, width), jnp.bfloat16)
    carried = [] if ladder is None else [ladder]
    results = pl.pallas_call(
        functools.partial(pack_kernel, first, rows),
        in_specs=[SMEM, SMEM, VMEM] + [ANY] * len(carried),
        out_specs=[ANY] + [VMEM] * SIDE,
        out_shape=[whole] + [piece] * SIDE,
        scratch_shapes=[pltpu.SMEM((slots,), jnp.int32), pltpu.SemaphoreType.DMA],
        input_output_aliases={3: 0} if carried else {},
        compiler_params=params(32),
        cost_estimate=cost(0, 8 * part.size),
        name="pack",
    )(place, crossing, part, *carried)
    return results[0], list(results[1:])


def collect_kernel(first, rows, ids_ref, other_ref, *rest):
    pieces, (out_ref, total, staged, sems) = rest[:SIDE], rest[-4:]
    window = slice(first, first + rows)
    read = pltpu.make_async_copy(other_ref.at[:, window], staged, sems.at[0])
    read.start()
    read.wait()
    total[...] = staged[...].astype(jnp.float32)
    for two in range(SIDE):
        for at in range(SIDE * CAP):
            target = ids_ref[two * SIDE * CAP + at]

            @pl.when(target >= 0)
            def _():
                total[target] += pieces[two][at].astype(jnp.float32)

    staged[...] = total[...].astype(jnp.bfloat16)
    write = pltpu.make_async_copy(staged, out_ref.at[:, window], sems.at[1])
    write.start()
    write.wait()


def collect(ids, other, pieces, crossed, first):
    q_local, freq, width = other.shape
    rows = pieces[0].shape[1]
    carried = [] if crossed is None else [crossed]
    return pl.pallas_call(
        functools.partial(collect_kernel, first, rows),
        in_specs=[SMEM, ANY] + [VMEM] * SIDE + [ANY] * len(carried),
        out_specs=ANY,
        out_shape=jax.ShapeDtypeStruct(other.shape, jnp.bfloat16),
        scratch_shapes=[
            pltpu.VMEM((q_local, rows, width), jnp.float32),
            pltpu.VMEM((q_local, rows, width), jnp.bfloat16),
            pltpu.SemaphoreType.DMA((2,)),
        ],
        input_output_aliases={2 + SIDE: 0} if carried else {},
        compiler_params=params(40),
        cost_estimate=cost(0, 16 * q_local * rows * width),
        name="collect",
    )(ids, other, *pieces, *carried)


def find_kernel(place_ref, everyone_ref, ids_ref, seen):
    q_local = everyone_ref.shape[2]
    for two in range(SIDE):
        for one in range(SIDE):
            slot = (two * SIDE + one) * CAP
            ids_ref[slot] = -1
            ids_ref[slot + 1] = -1
            seen[0] = slot

            @pl.loop(0, q_local)
            def _(index):
                value = everyone_ref[two, one, index]

                @pl.when(value // q_local == place_ref[3])
                def _():
                    ids_ref[seen[0]] = value % q_local
                    seen[0] = slot + 1


def arriving(place, crossing):
    row = jnp.stack([crossing] + [shift(crossing, step, 0) for step in range(1, SIDE)])
    everyone = jnp.stack([row] + [shift(row, step, 1) for step in range(1, SIDE)])
    return pl.pallas_call(
        find_kernel,
        in_specs=[SMEM, SMEM],
        out_specs=SMEM,
        out_shape=jax.ShapeDtypeStruct((CAP * SIDE * SIDE,), jnp.int32),
        scratch_shapes=[pltpu.SMEM((1,), jnp.int32)],
        name="find",
    )(place, everyone)


def shift(value, step, phase):
    n_row = lax.axis_size("row")
    pairs = []
    for x in range(SIDE):
        for y in range(SIDE):
            for row in range(n_row):
                if row % 2 == phase:
                    target = (x + step) % SIDE * SIDE + y
                else:
                    target = x * SIDE + (y + step) % SIDE
                pairs.append(((x * SIDE + y) * n_row + row, target * n_row + row))
    return lax.ppermute(value, ("boson", "row"), pairs)


def regroup_kernel(*refs):
    for two in range(SIDE):
        for one in range(SIDE):
            refs[SIDE + two][one * CAP : one * CAP + CAP] = refs[one][two * CAP : two * CAP + CAP]


def regroup(pieces):
    shape = jax.ShapeDtypeStruct(pieces[0].shape, pieces[0].dtype)
    return pl.pallas_call(
        regroup_kernel,
        in_specs=[VMEM] * SIDE,
        out_specs=[VMEM] * SIDE,
        out_shape=[shape] * SIDE,
        compiler_params=params(32),
        cost_estimate=cost(0, 4 * SIDE * pieces[0].size),
        name="regroup",
    )(*pieces)


def after(value, *earlier):
    return lax.optimization_barrier((value, *earlier))[0]


def spread(pieces, phase):
    moved = {step: shift(pieces[step], step, phase) for step in (1, 3, 2)}
    return [pieces[0]] + [moved[step] for step in range(1, SIDE)]


def exchange(pieces, earlier=()):
    again = regroup(spread(pieces, 0))
    if earlier:
        again, _ = lax.optimization_barrier((again, earlier))
    return spread(again, 1), again[1]


def local(vertex, bubble, vertex_cross, crossing):
    n_row = lax.axis_size("row")
    q_local, freq, width = vertex.shape
    mine = q_local // n_row
    me = lax.axis_index("boson")
    odd = lax.axis_index("row") % 2
    high, low = me // SIDE, me % SIDE
    place = jnp.stack([jnp.where(odd == 1, low, high), jnp.where(odd == 1, high, low), odd, me]).astype(jnp.int32)
    crossing = crossing.reshape(q_local)
    ids = arriving(place, crossing)
    whole = lax.all_to_all(
        vertex.reshape(n_row, mine, freq, width), "row", split_axis=0, concat_axis=0, tiled=True
    )
    scales = lax.dynamic_slice_in_dim(bubble, lax.axis_index("row") * mine, mine, 0)
    whole, scales, ids = lax.optimization_barrier((whole, scales, ids))
    ladder = None
    packed, summed, halfway = [], [], ()
    firsts = [sum(CHUNKS[:step]) for step in range(len(CHUNKS))]
    ready = {step: sweeps(whole, scales, firsts[step], rows) for step, rows in enumerate(CHUNKS)}
    for step, rows in enumerate(CHUNKS):
        first, solved = firsts[step], ready[step]
        if step >= 1:
            solved = after(solved, packed[step - 1])
        if step >= 2:
            solved, summed[step - 2] = lax.optimization_barrier((solved, summed[step - 2]))
        part = lax.all_to_all(solved, "row", split_axis=0, concat_axis=0, tiled=True)
        part = part.reshape(q_local, rows, width)
        part = after(part, *halfway)
        if step == 0:
            for other in range(1, min(AHEAD, len(CHUNKS))):
                part, ready[other] = lax.optimization_barrier((part, ready[other]))
        ladder, outgoing = pack(place, crossing, part, ladder, first, freq)
        packed.append(outgoing[1])
        pieces, half = exchange(outgoing, summed[step - 1 : step])
        halfway = (half,)
        summed.append(collect(ids, vertex_cross, pieces, summed[-1] if summed else None, first))
    return ladder, summed[-1]


def solution(mesh):
    placed = (P("boson", "row", None), P("boson", None), P("boson", "row", None), P("boson", "row"))
    return jax.shard_map(
        local,
        mesh=mesh,
        in_specs=placed,
        out_specs=(P("boson", "row", None), P("boson", "row", None)),
        check_vma=False,
    )
```

```python
import functools

import jax
import jax.numpy as jnp
from jax import lax
from jax.experimental import pallas as pl
from jax.experimental.pallas import tpu as pltpu
from jax.sharding import PartitionSpec as P

CAP = 2
ITERS = 6
SIDE = 4
SWEEP_MIB = 24
PACK_MIB = 12
GROUP_MIB = 12
CHUNKS = (32, 48, 48)
VMEM = pl.BlockSpec(memory_space=pltpu.VMEM)
SMEM = pl.BlockSpec(memory_space=pltpu.SMEM)
HBM = pl.BlockSpec(memory_space=pltpu.HBM)
TOKEN = jax.ShapeDtypeStruct((8, 128), jnp.float32)


def params(mib):
    return pltpu.CompilerParams(vmem_limit_bytes=mib << 20)


def cost(flops, nbytes):
    return pl.CostEstimate(flops=int(flops), bytes_accessed=int(nbytes), transcendentals=0)


def sweep_kernel(first, rows, vertex_ref, bubble_ref, *rest):
    ladder_ref, matrices, results, sems = rest[-4:]
    blocks, count, freq, width = vertex_ref.shape
    reads = [
        pltpu.make_async_copy(vertex_ref.at[:, index], matrices.at[index], sems.at[0, index])
        for index in range(count)
    ]
    writes = [
        pltpu.make_async_copy(results.at[index], ladder_ref.at[:, index], sems.at[1, index])
        for index in range(count)
    ]
    for read in reads:
        read.start()
    for index in range(count):
        reads[index].wait()
        scales = bubble_ref[index : index + 1, :]
        start = matrices[index, :, first : first + rows].reshape(blocks * rows, width).astype(jnp.float32)
        current = start
        for _ in range(ITERS):
            scaled = (current * scales).astype(jnp.bfloat16)
            matrix = matrices[index].reshape(blocks * freq, width)
            current = start + jnp.dot(scaled, matrix, preferred_element_type=jnp.float32)
        results[index] = current.astype(jnp.bfloat16).reshape(blocks, rows, width)
        writes[index].start()
    for write in writes:
        write.wait()


def sweeps(vertex, bubble, first, rows, earlier=()):
    blocks, count, freq, width = vertex.shape
    return pl.pallas_call(
        functools.partial(sweep_kernel, first, rows),
        in_specs=[HBM, VMEM] + [HBM] * len(earlier),
        out_specs=HBM,
        out_shape=jax.ShapeDtypeStruct((blocks, count, rows, width), jnp.bfloat16),
        scratch_shapes=[
            pltpu.VMEM((count, blocks, freq, width), jnp.bfloat16),
            pltpu.VMEM((count, blocks, rows, width), jnp.bfloat16),
            pltpu.SemaphoreType.DMA((2, count)),
        ],
        compiler_params=params(SWEEP_MIB),
        cost_estimate=cost(2 * ITERS * count * blocks * rows * width * width, 2 * vertex.size),
        name="sweeps",
    )(vertex, bubble, *earlier)


def pack_kernel(first, rows, place_ref, crossing_ref, part_ref, *rest):
    ladder_ref, outs, token, used, sem = rest[-SIDE - 4], rest[-SIDE - 3 : -3], rest[-3], rest[-2], rest[-1]
    token[...] = jnp.zeros_like(token)
    q_local = part_ref.shape[0]
    keep = pltpu.make_async_copy(part_ref, ladder_ref.at[:, first : first + rows], sem)
    keep.start()
    for slot in range(SIDE * SIDE * CAP):
        used[slot] = -1
    for index in range(q_local):
        target = crossing_ref[index] // q_local
        high, low = target // SIDE, target % SIDE
        swap = place_ref[2] == 1
        one = (jnp.where(swap, low, high) - place_ref[0] + SIDE) % SIDE
        two = (jnp.where(swap, high, low) - place_ref[1] + SIDE) % SIDE
        slot = (one * SIDE + two) * CAP
        slot = jnp.where(used[slot] < 0, slot, slot + 1)
        used[slot] = index
    for one in range(SIDE):
        for at in range(SIDE * CAP):
            index = used[one * SIDE * CAP + at]

            @pl.when(index >= 0)
            def _():
                outs[one][at] = part_ref[index]

    keep.wait()


def pack(place, crossing, part, ladder, first, freq, earlier=()):
    q_local, rows, width = part.shape
    slots = SIDE * SIDE * CAP
    whole = jax.ShapeDtypeStruct((q_local, freq, width), jnp.bfloat16)
    piece = jax.ShapeDtypeStruct((SIDE * CAP, rows, width), jnp.bfloat16)
    carried = [] if ladder is None else [ladder]
    results = pl.pallas_call(
        functools.partial(pack_kernel, first, rows),
        in_specs=[SMEM, SMEM, VMEM] + [HBM] * (len(carried) + len(earlier)),
        out_specs=[HBM] + [VMEM] * (SIDE + 1),
        out_shape=[whole] + [piece] * SIDE + [TOKEN],
        scratch_shapes=[pltpu.SMEM((slots,), jnp.int32), pltpu.SemaphoreType.DMA],
        input_output_aliases={3: 0} if carried else {},
        compiler_params=params(PACK_MIB),
        cost_estimate=cost(0, 8 * part.size),
        name="pack",
    )(place, crossing, part, *carried, *earlier)
    return results[0], list(results[1:-1]), results[-1]


def collect_kernel(first, rows, ids_ref, other_ref, *rest):
    pieces, (out_ref, total, staged, sems) = rest[:SIDE], rest[-4:]
    window = slice(first, first + rows)
    read = pltpu.make_async_copy(other_ref.at[:, window], staged, sems.at[0])
    read.start()
    read.wait()
    total[...] = staged[...].astype(jnp.float32)
    for two in range(SIDE):
        for at in range(SIDE * CAP):
            target = ids_ref[two * SIDE * CAP + at]

            @pl.when(target >= 0)
            def _():
                total[target] += pieces[two][at].astype(jnp.float32)

    staged[...] = total[...].astype(jnp.bfloat16)
    write = pltpu.make_async_copy(staged, out_ref.at[:, window], sems.at[1])
    write.start()
    write.wait()


def collect(ids, other, pieces, crossed, first, earlier=()):
    q_local, freq, width = other.shape
    rows = pieces[0].shape[1]
    return pl.pallas_call(
        functools.partial(collect_kernel, first, rows),
        in_specs=[SMEM, HBM] + [VMEM] * SIDE + [HBM] * (len(crossed) + len(earlier)),
        out_specs=HBM,
        out_shape=jax.ShapeDtypeStruct(other.shape, jnp.bfloat16),
        scratch_shapes=[
            pltpu.VMEM((q_local, rows, width), jnp.float32),
            pltpu.VMEM((q_local, rows, width), jnp.bfloat16),
            pltpu.SemaphoreType.DMA((2,)),
        ],
        input_output_aliases={2 + SIDE: 0} if crossed else {},
        compiler_params=params(16),
        cost_estimate=cost(0, 16 * q_local * rows * width),
        name="collect",
    )(ids, other, *pieces, *crossed, *earlier)


def find_kernel(place_ref, everyone_ref, ids_ref, seen):
    q_local = everyone_ref.shape[2]
    for two in range(SIDE):
        for one in range(SIDE):
            slot = (two * SIDE + one) * CAP
            ids_ref[slot] = -1
            ids_ref[slot + 1] = -1
            seen[0] = slot

            @pl.loop(0, q_local)
            def _(index):
                value = everyone_ref[two, one, index]

                @pl.when(value // q_local == place_ref[3])
                def _():
                    ids_ref[seen[0]] = value % q_local
                    seen[0] = slot + 1


def arriving(place, crossing):
    row = jnp.stack([crossing] + [shift(crossing, step, 0) for step in range(1, SIDE)])
    everyone = jnp.stack([row] + [shift(row, step, 1) for step in range(1, SIDE)])
    return pl.pallas_call(
        find_kernel,
        in_specs=[SMEM, SMEM],
        out_specs=SMEM,
        out_shape=jax.ShapeDtypeStruct((CAP * SIDE * SIDE,), jnp.int32),
        scratch_shapes=[pltpu.SMEM((1,), jnp.int32)],
        name="find",
    )(place, everyone)


def shift(value, step, phase):
    n_row = lax.axis_size("row")
    pairs = []
    for x in range(SIDE):
        for y in range(SIDE):
            for row in range(n_row):
                if row % 2 == phase:
                    target = (x + step) % SIDE * SIDE + y
                else:
                    target = x * SIDE + (y + step) % SIDE
                pairs.append(((x * SIDE + y) * n_row + row, target * n_row + row))
    return lax.ppermute(value, ("boson", "row"), pairs)


def regroup_kernel(*refs):
    pieces, outs, token = refs[:SIDE], refs[-SIDE - 1 : -1], refs[-1]
    token[...] = jnp.zeros_like(token)
    for two in range(SIDE):
        for one in range(SIDE):
            outs[two][one * CAP : one * CAP + CAP] = pieces[one][two * CAP : two * CAP + CAP]


def regroup(pieces, earlier=()):
    shape = jax.ShapeDtypeStruct(pieces[0].shape, pieces[0].dtype)
    return pl.pallas_call(
        regroup_kernel,
        in_specs=[VMEM] * SIDE + [HBM] * len(earlier),
        out_specs=[VMEM] * (SIDE + 1),
        out_shape=[shape] * SIDE + [TOKEN],
        compiler_params=params(GROUP_MIB),
        cost_estimate=cost(0, 4 * SIDE * pieces[0].size),
        name="regroup",
    )(*pieces, *earlier)


def after(value, *earlier):
    return lax.optimization_barrier((value, *earlier))[0]


def spread(pieces, phase):
    moved = {step: shift(pieces[step], step, phase) for step in (1, 3, 2)}
    return [pieces[0]] + [moved[step] for step in range(1, SIDE)]


def local(vertex, bubble, vertex_cross, crossing):
    n_row = lax.axis_size("row")
    q_local, freq, width = vertex.shape
    mine = q_local // n_row
    me = lax.axis_index("boson")
    odd = lax.axis_index("row") % 2
    high, low = me // SIDE, me % SIDE
    place = jnp.stack([jnp.where(odd == 1, low, high), jnp.where(odd == 1, high, low), odd, me]).astype(jnp.int32)
    crossing = crossing.reshape(q_local)
    ids = arriving(place, crossing)
    whole = lax.all_to_all(
        vertex.reshape(n_row, mine, freq, width), "row", split_axis=0, concat_axis=0, tiled=True
    )
    scales = lax.dynamic_slice_in_dim(bubble, lax.axis_index("row") * mine, mine, 0)
    whole, scales, ids = lax.optimization_barrier((whole, scales, ids))
    firsts = [sum(CHUNKS[:step]) for step in range(len(CHUNKS))]
    chunks = list(zip(firsts, CHUNKS))

    def back(solved, rows):
        part = lax.all_to_all(solved, "row", split_axis=0, concat_axis=0, tiled=True)
        return part.reshape(q_local, rows, width)

    solved = [sweeps(whole, scales, *chunk) for chunk in chunks[:2]]
    ladder, crossed, arrived, halfway = None, [], [], []
    for step, (first, rows) in enumerate(chunks):
        part = back(solved[step], rows)
        ladder, outgoing, token = pack(
            place, crossing, part, ladder, first, freq, (solved[1:] if step == 0 else []) + halfway
        )
        ahead = [sweeps(whole, scales, *chunk, [token]) for chunk in chunks[step + 2 : step + 3]]
        solved += ahead
        moved = spread(outgoing, 0)
        *again, token = regroup(moved, ahead + arrived[1:])
        halfway = [token]
        if arrived:
            crossed = [collect(ids, vertex_cross, arrived, crossed, firsts[step - 1], halfway)]
        arrived = spread(again, 1)
    return ladder, collect(ids, vertex_cross, arrived, crossed, firsts[-1])


def solution(mesh):
    placed = (P("boson", "row", None), P("boson", None), P("boson", "row", None), P("boson", "row"))
    return jax.shard_map(
        local,
        mesh=mesh,
        in_specs=placed,
        out_specs=(P("boson", "row", None), P("boson", "row", None)),
        check_vma=False,
    )
```

```python
import functools

import jax
import jax.numpy as jnp
from jax import lax
from jax.experimental import pallas as pl
from jax.experimental.pallas import tpu as pltpu
from jax.sharding import PartitionSpec as P

CAP = 2
ITERS = 6
SIDE = 4
PARTS = 4
SWEEP_MIB = 24
PACK_MIB = 12
GROUP_MIB = 12
CHUNKS = (32, 48, 48)
VMEM = pl.BlockSpec(memory_space=pltpu.VMEM)
SMEM = pl.BlockSpec(memory_space=pltpu.SMEM)
HBM = pl.BlockSpec(memory_space=pltpu.HBM)
TOKEN = jax.ShapeDtypeStruct((8, 128), jnp.float32)


def params(mib):
    return pltpu.CompilerParams(vmem_limit_bytes=mib << 20)


def cost(flops, nbytes):
    return pl.CostEstimate(flops=int(flops), bytes_accessed=int(nbytes), transcendentals=0)


def sweep_kernel(first, rows, vertex_ref, bubble_ref, *rest):
    ladder_ref, matrices, results, sems = rest[-4:]
    blocks, count, freq, width = vertex_ref.shape
    reads = [
        pltpu.make_async_copy(vertex_ref.at[:, index], matrices.at[index], sems.at[0, index])
        for index in range(count)
    ]
    writes = [
        pltpu.make_async_copy(results.at[index], ladder_ref.at[:, index], sems.at[1, index])
        for index in range(count)
    ]
    for read in reads:
        read.start()
    for index in range(count):
        reads[index].wait()
        scales = bubble_ref[index : index + 1, :]
        start = matrices[index, :, first : first + rows].reshape(blocks * rows, width).astype(jnp.float32)
        current = start
        for _ in range(ITERS):
            scaled = (current * scales).astype(jnp.bfloat16)
            matrix = matrices[index].reshape(blocks * freq, width)
            current = start + jnp.dot(scaled, matrix, preferred_element_type=jnp.float32)
        results[index] = current.astype(jnp.bfloat16).reshape(blocks, rows, width)
        writes[index].start()
    for write in writes:
        write.wait()


def sweeps(vertex, bubble, first, rows, earlier=()):
    blocks, count, freq, width = vertex.shape
    return pl.pallas_call(
        functools.partial(sweep_kernel, first, rows),
        in_specs=[HBM, VMEM] + [HBM] * len(earlier),
        out_specs=HBM,
        out_shape=jax.ShapeDtypeStruct((blocks, count, rows, width), jnp.bfloat16),
        scratch_shapes=[
            pltpu.VMEM((count, blocks, freq, width), jnp.bfloat16),
            pltpu.VMEM((count, blocks, rows, width), jnp.bfloat16),
            pltpu.SemaphoreType.DMA((2, count)),
        ],
        compiler_params=params(SWEEP_MIB),
        cost_estimate=cost(2 * ITERS * count * blocks * rows * width * width, 2 * vertex.size),
        name="sweeps",
    )(vertex, bubble, *earlier)


def pack_kernel(first, rows, place_ref, crossing_ref, part_ref, *rest):
    ladder_ref, outs, token, used, sem = rest[-SIDE - 4], rest[-SIDE - 3 : -3], rest[-3], rest[-2], rest[-1]
    token[...] = jnp.zeros_like(token)
    q_local = part_ref.shape[0]
    keep = pltpu.make_async_copy(part_ref, ladder_ref.at[:, first : first + rows], sem)
    keep.start()
    for slot in range(SIDE * SIDE * CAP):
        used[slot] = -1
    for index in range(q_local):
        target = crossing_ref[index] // q_local
        high, low = target // SIDE, target % SIDE
        swap = place_ref[2] == 1
        one = (jnp.where(swap, low, high) - place_ref[0] + SIDE) % SIDE
        two = (jnp.where(swap, high, low) - place_ref[1] + SIDE) % SIDE
        slot = (one * SIDE + two) * CAP
        slot = jnp.where(used[slot] < 0, slot, slot + 1)
        used[slot] = index
    for one in range(SIDE):
        for at in range(SIDE * CAP):
            index = used[one * SIDE * CAP + at]

            @pl.when(index >= 0)
            def _():
                outs[one][at] = part_ref[index]

    keep.wait()


def pack(place, crossing, part, ladder, first, freq, earlier=()):
    q_local, rows, width = part.shape
    slots = SIDE * SIDE * CAP
    whole = jax.ShapeDtypeStruct((q_local, freq, width), jnp.bfloat16)
    piece = jax.ShapeDtypeStruct((SIDE * CAP, rows, width), jnp.bfloat16)
    carried = [] if ladder is None else [ladder]
    results = pl.pallas_call(
        functools.partial(pack_kernel, first, rows),
        in_specs=[SMEM, SMEM, VMEM] + [HBM] * (len(carried) + len(earlier)),
        out_specs=[HBM] + [VMEM] * (SIDE + 1),
        out_shape=[whole] + [piece] * SIDE + [TOKEN],
        scratch_shapes=[pltpu.SMEM((slots,), jnp.int32), pltpu.SemaphoreType.DMA],
        input_output_aliases={3: 0} if carried else {},
        compiler_params=params(PACK_MIB),
        cost_estimate=cost(0, 8 * part.size),
        name="pack",
    )(place, crossing, part, *carried, *earlier)
    return results[0], list(results[1:-1]), results[-1]


def collect_kernel(first, rows, ids_ref, other_ref, *rest):
    pieces, (out_ref, total, staged, sems) = rest[:SIDE], rest[-4:]
    window = slice(first, first + rows)
    share = staged.shape[0] // PARTS
    spans = [slice(part * share, part * share + share) for part in range(PARTS)]
    reads = [pltpu.make_async_copy(other_ref.at[q, window], staged.at[q], sems.at[0, i]) for i, q in enumerate(spans)]
    writes = [pltpu.make_async_copy(staged.at[q], out_ref.at[q, window], sems.at[1, i]) for i, q in enumerate(spans)]
    for read in reads:
        read.start()
    for read, span in zip(reads, spans):
        read.wait()
        total[span] = staged[span].astype(jnp.float32)
    for two in range(SIDE):
        for at in range(SIDE * CAP):
            target = ids_ref[two * SIDE * CAP + at]

            @pl.when(target >= 0)
            def _():
                total[target] += pieces[two][at].astype(jnp.float32)

    for write, span in zip(writes, spans):
        staged[span] = total[span].astype(jnp.bfloat16)
        write.start()
    for write in writes:
        write.wait()


def collect(ids, other, pieces, crossed, first, earlier=()):
    q_local, freq, width = other.shape
    rows = pieces[0].shape[1]
    return pl.pallas_call(
        functools.partial(collect_kernel, first, rows),
        in_specs=[SMEM, HBM] + [VMEM] * SIDE + [HBM] * (len(crossed) + len(earlier)),
        out_specs=HBM,
        out_shape=jax.ShapeDtypeStruct(other.shape, jnp.bfloat16),
        scratch_shapes=[
            pltpu.VMEM((q_local, rows, width), jnp.float32),
            pltpu.VMEM((q_local, rows, width), jnp.bfloat16),
            pltpu.SemaphoreType.DMA((2, PARTS)),
        ],
        input_output_aliases={2 + SIDE: 0} if crossed else {},
        compiler_params=params(16),
        cost_estimate=cost(0, 16 * q_local * rows * width),
        name="collect",
    )(ids, other, *pieces, *crossed, *earlier)


def find_kernel(place_ref, everyone_ref, ids_ref, seen):
    q_local = everyone_ref.shape[2]
    for two in range(SIDE):
        for one in range(SIDE):
            slot = (two * SIDE + one) * CAP
            ids_ref[slot] = -1
            ids_ref[slot + 1] = -1
            seen[0] = slot

            @pl.loop(0, q_local)
            def _(index):
                value = everyone_ref[two, one, index]

                @pl.when(value // q_local == place_ref[3])
                def _():
                    ids_ref[seen[0]] = value % q_local
                    seen[0] = slot + 1


def arriving(place, crossing):
    row = jnp.stack([crossing] + [shift(crossing, step, 0) for step in range(1, SIDE)])
    everyone = jnp.stack([row] + [shift(row, step, 1) for step in range(1, SIDE)])
    return pl.pallas_call(
        find_kernel,
        in_specs=[SMEM, SMEM],
        out_specs=SMEM,
        out_shape=jax.ShapeDtypeStruct((CAP * SIDE * SIDE,), jnp.int32),
        scratch_shapes=[pltpu.SMEM((1,), jnp.int32)],
        name="find",
    )(place, everyone)


def shift(value, step, phase):
    n_row = lax.axis_size("row")
    pairs = []
    for x in range(SIDE):
        for y in range(SIDE):
            for row in range(n_row):
                if row % 2 == phase:
                    target = (x + step) % SIDE * SIDE + y
                else:
                    target = x * SIDE + (y + step) % SIDE
                pairs.append(((x * SIDE + y) * n_row + row, target * n_row + row))
    return lax.ppermute(value, ("boson", "row"), pairs)


def regroup_kernel(*refs):
    pieces, outs, token = refs[:SIDE], refs[-SIDE - 1 : -1], refs[-1]
    token[...] = jnp.zeros_like(token)
    for two in range(SIDE):
        for one in range(SIDE):
            outs[two][one * CAP : one * CAP + CAP] = pieces[one][two * CAP : two * CAP + CAP]


def regroup(pieces, earlier=()):
    shape = jax.ShapeDtypeStruct(pieces[0].shape, pieces[0].dtype)
    return pl.pallas_call(
        regroup_kernel,
        in_specs=[VMEM] * SIDE + [HBM] * len(earlier),
        out_specs=[VMEM] * (SIDE + 1),
        out_shape=[shape] * SIDE + [TOKEN],
        compiler_params=params(GROUP_MIB),
        cost_estimate=cost(0, 4 * SIDE * pieces[0].size),
        name="regroup",
    )(*pieces, *earlier)


def after(value, *earlier):
    return lax.optimization_barrier((value, *earlier))[0]


def spread(pieces, phase):
    moved = {step: shift(pieces[step], step, phase) for step in (1, 3, 2)}
    return [pieces[0]] + [moved[step] for step in range(1, SIDE)]


def local(vertex, bubble, vertex_cross, crossing):
    n_row = lax.axis_size("row")
    q_local, freq, width = vertex.shape
    mine = q_local // n_row
    me = lax.axis_index("boson")
    odd = lax.axis_index("row") % 2
    high, low = me // SIDE, me % SIDE
    place = jnp.stack([jnp.where(odd == 1, low, high), jnp.where(odd == 1, high, low), odd, me]).astype(jnp.int32)
    crossing = crossing.reshape(q_local)
    ids = arriving(place, crossing)
    whole = lax.all_to_all(
        vertex.reshape(n_row, mine, freq, width), "row", split_axis=0, concat_axis=0, tiled=True
    )
    scales = lax.dynamic_slice_in_dim(bubble, lax.axis_index("row") * mine, mine, 0)
    whole, scales, ids = lax.optimization_barrier((whole, scales, ids))
    firsts = [sum(CHUNKS[:step]) for step in range(len(CHUNKS))]
    chunks = list(zip(firsts, CHUNKS))

    def back(solved, rows):
        part = lax.all_to_all(solved, "row", split_axis=0, concat_axis=0, tiled=True)
        return part.reshape(q_local, rows, width)

    solved = [sweeps(whole, scales, *chunk) for chunk in chunks[:2]]
    ladder, crossed, arrived, halfway = None, [], [], []
    for step, (first, rows) in enumerate(chunks):
        part = back(solved[step], rows)
        ladder, outgoing, token = pack(
            place, crossing, part, ladder, first, freq, (solved[1:] if step == 0 else []) + halfway
        )
        ahead = [sweeps(whole, scales, *chunk, [token]) for chunk in chunks[step + 2 : step + 3]]
        solved += ahead
        moved = spread(outgoing, 0)
        *again, token = regroup(moved, ahead + arrived[1:])
        halfway = [token]
        if arrived:
            crossed = [collect(ids, vertex_cross, arrived, crossed, firsts[step - 1], halfway)]
        arrived = spread(again, 1)
    return ladder, collect(ids, vertex_cross, arrived, crossed, firsts[-1])


def solution(mesh):
    placed = (P("boson", "row", None), P("boson", None), P("boson", "row", None), P("boson", "row"))
    return jax.shard_map(
        local,
        mesh=mesh,
        in_specs=placed,
        out_specs=(P("boson", "row", None), P("boson", "row", None)),
        check_vma=False,
    )
```
